32 devices in a mesh: row: 4 (over z), col: 8 (over y, x, core).
Axes of the slice: x: 2, y: 2, z: 4, core: 2. Of those that a mesh axis runs over, the one named last changes fastest.
Arguments:
- features: bfloat16 [6144, 512], P(('col', 'row')), may hold values from -6 to 6
- out_grad: bfloat16 [6144, 512], P(('row', 'col')), may hold values from -6 to 6
- weight: bfloat16 [512, 512], replicated, may hold values from -0.25 to 0.25
- block_values: bfloat16 [4, 8, 72, 4096], P('row', 'col'), may hold values from -0.25 to 0.25
- block_coords: int32 [4, 8, 2, 72], P('row', 'col'), may hold values from 0 to 23, as said below
- block_counts: int32 [4, 8], P('row', 'col'), may hold values from 1 to 72, as said below
Outputs:
- activations: bfloat16 [6144, 512], P(('row', 'col'))
- weight_grad: float32 [512, 512], replicated
- feature_grad: bfloat16 [6144, 512], P(('col', 'row'))
The draws below stay inside these ranges and needn't reach their ends.
Inputs may be any that keep to these rules, and one draw needn't show every extreme that they name: `block_coords`: entry 0 of a slot is a block row below 24, entry 1 a block column below 12; the 72 slots of a tile name distinct blocks. `block_counts`: slots from the count onward are padding: their coordinates and values are ignored. Some tile has exactly 72 live slots.
All inputs are finite; a program needn't handle non-finite values.
Results may differ from the reference program's by a relative error of at most 0.025.
Values may be sent and summed in bfloat16 or wider, within the bound.
A program may use at most 128 MiB of HBM per device.

```python
import math
import jax
import jax.numpy as jnp
from jax import lax

D = 512
BLOCK = 64
NODES = 6144
BR = 24
BC = 12
MAXB = 72
N_ROW = 4
N_COL = 8


def draw_block_coords(key, part):
    tiles = N_ROW * N_COL
    keys = jax.random.split(jax.random.fold_in(key, 11), tiles)
    orders = jax.vmap(lambda single: jax.random.permutation(single, BR * BC))(keys)[:, :MAXB]
    stacked = jnp.stack([orders // BC, orders % BC], axis=1)
    return stacked.reshape(N_ROW, N_COL, 2, MAXB).astype(jnp.int32)


def draw_block_counts(key, part):
    tiles = N_ROW * N_COL
    first_key, second_key, third_key = jax.random.split(jax.random.fold_in(key, 23), 3)
    first = jax.random.randint(first_key, (tiles,), 1, MAXB + 1)
    second = jax.random.randint(second_key, (tiles,), 1, MAXB + 1)
    chosen = jax.random.randint(third_key, (), 0, tiles)
    counts = jnp.minimum(first, second)
    counts = jnp.where(jnp.arange(tiles) == chosen, MAXB, counts)
    return counts.reshape(N_ROW, N_COL).astype(jnp.int32)


def block_levels(rng, dims, pieces, low, high):
    loudness = 1.0
    for position, blocks in pieces:
        heights = jax.random.uniform(jax.random.fold_in(jax.random.fold_in(rng, 6), position), (blocks,), jnp.float32, low / len(pieces), high / len(pieces))
        loudness = loudness * jnp.repeat(jnp.exp(heights), dims[position] // blocks).reshape((-1,) + (1,) * (len(dims) - 1 - position))
    return loudness


def centred(rng, shape, width, bound, cuts=(), kind=jnp.bfloat16):
    array = width * jax.random.normal(rng, shape, jnp.float32)
    if cuts:
        array = array * block_levels(rng, shape, cuts, -0.22, 0.18)
    return jnp.clip(array, -bound, bound).astype(kind)


def setup_inputs(seed: int = 0) -> dict:
    seeds = jax.random.split(jax.random.key(seed), 7)
    return {
        "features": centred(seeds[0], (NODES, D), 1.0, 6.0, ((0, 32),)),
        "out_grad": centred(seeds[1], (NODES, D), 1.0, 6.0, ((0, 32),)),
        "weight": centred(seeds[2], (D, D), D ** -0.5, 0.25),
        "block_values": centred(seeds[3], (N_ROW, N_COL, MAXB, BLOCK * BLOCK), (NODES // 12) ** -0.5, 0.25, ((0, 4), (1, 8))),
        "block_coords": draw_block_coords(jax.random.fold_in(seeds[6], 71), 0),
        "block_counts": draw_block_counts(jax.random.fold_in(seeds[6], 71), 0),
    }


def forward_tile(slot_vals, coords, panel):
    panel_blocks = panel.reshape(BC, BLOCK, D).astype(jnp.float32)
    gathered = panel_blocks[coords[1]]
    products = jnp.einsum('mrc,mcd->mrd', slot_vals, gathered)
    totals = jnp.zeros((BR, BLOCK, D), jnp.float32).at[coords[0]].add(products)
    return totals.reshape(BR * BLOCK, D)

def backward_tile(slot_vals, coords, grad_rows):
    grad_blocks = grad_rows.reshape(BR, BLOCK, D).astype(jnp.float32)
    gathered = grad_blocks[coords[0]]
    products = jnp.einsum('mrc,mrd->mcd', slot_vals, gathered)
    totals = jnp.zeros((BC, BLOCK, D), jnp.float32).at[coords[1]].add(products)
    return totals.reshape(BC * BLOCK, D)

def reference(features, out_grad, weight, block_values, block_coords, block_counts):
    all_vals = block_values.astype(jnp.float32).reshape(N_ROW, N_COL, MAXB, BLOCK, BLOCK)
    live = jnp.arange(MAXB, dtype=jnp.int32)[None, None, :] < block_counts[:, :, None]
    all_vals = jnp.where(live[:, :, :, None, None], all_vals, jnp.float32(0.0))
    panels = features.reshape(N_COL, BC * BLOCK, D)

    def forward_row(i):

        def advance(totals, j):
            piece = forward_tile(all_vals[i, j], block_coords[i, j], panels[j])
            return (totals + piece.astype(jnp.bfloat16).astype(jnp.float32), None)
        totals, _ = lax.scan(advance, jnp.zeros((BR * BLOCK, D), jnp.float32), jnp.arange(N_COL, dtype=jnp.int32))
        return totals.astype(jnp.bfloat16)
    aggregated = lax.map(forward_row, jnp.arange(N_ROW, dtype=jnp.int32)).reshape(NODES, D)
    pre_act = jnp.dot(aggregated, weight, preferred_element_type=jnp.float32)
    sigmoid_pre = jax.nn.sigmoid(pre_act)
    activations = (pre_act * sigmoid_pre).astype(jnp.bfloat16)
    grad_pre = (out_grad.astype(jnp.float32) * sigmoid_pre * (1.0 + pre_act * (1.0 - sigmoid_pre))).astype(jnp.bfloat16)
    weight_grad = lax.dot_general(aggregated, grad_pre, (((0,), (0,)), ((), ())), preferred_element_type=jnp.float32)
    weight_grad = weight_grad * jnp.float32(1.0 / math.sqrt(NODES))
    grad_agg = lax.dot_general(grad_pre, weight, (((1,), (1,)), ((), ())), preferred_element_type=jnp.float32).astype(jnp.bfloat16)
    grad_rows = grad_agg.reshape(N_ROW, BR * BLOCK, D)

    def backward_col(j):

        def advance(totals, i):
            piece = backward_tile(all_vals[i, j], block_coords[i, j], grad_rows[i])
            return (totals + piece.astype(jnp.bfloat16).astype(jnp.float32), None)
        totals, _ = lax.scan(advance, jnp.zeros((BC * BLOCK, D), jnp.float32), jnp.arange(N_ROW, dtype=jnp.int32))
        return totals.astype(jnp.bfloat16)
    feature_grad = lax.map(backward_col, jnp.arange(N_COL, dtype=jnp.int32)).reshape(NODES, D)
    return (activations, weight_grad, feature_grad)
```

```python
import functools
import math

import jax
import jax.numpy as jnp
from jax import lax
from jax.experimental import pallas as pl
from jax.experimental.pallas import tpu as pltpu
from jax.sharding import PartitionSpec as P

SIDE = 64
CHUNKS = 2
F32 = jnp.float32
BF16 = jnp.bfloat16


def kernel(
    R, C, scale,
    slot_ref, feat_ref, og_ref, w_ref, vals_ref,
    act_ref, wgrad_ref, fgrad_ref,
    dense, dense_t, panel, own, a_send, a_recv, b_send, b_recv, agg_ref, gpre_ref,
    gfull, f_send, f_recv, wg, wa_send, wa_recv, wb_send, wb_recv, wz, wfull,
    feat_ss, feat_rs, a_ss, a_rs, b_ss, b_rs, g_ss, g_rs, gs_ss, gs_rs, f_ss, f_rs,
    wa_ss, wa_rs, wb_ss, wb_rs, wz_ss, wz_rs, wh_ss, wh_rs, ws_ss, ws_rs,
):
    K = CHUNKS
    rows, width = feat_ref.shape
    dc = width // K
    NC = C // 2
    r = lax.axis_index("row")
    c = lax.axis_index("col")
    chip = c // 2
    core = c % 2
    other = 1 - core
    sib = 2 * chip + other
    brows = rows * C // SIDE
    bcols = rows * R // SIDE

    def row_peer(d):
        return (r + d) % R

    def chip_peer(d):
        return 2 * ((chip + d) % NC) + core

    def remote(src, dst, ss, rs, axis, peer):
        return pltpu.make_async_remote_copy(
            src_ref=src, dst_ref=dst, send_sem=ss, recv_sem=rs,
            device_id={axis: peer}, device_id_type=pl.DeviceIdType.MESH,
        )

    barrier = pltpu.get_barrier_semaphore()
    for d in range(1, R):
        pl.semaphore_signal(barrier, inc=1, device_id={"row": row_peer(d)},
                            device_id_type=pl.DeviceIdType.MESH)
    for d in range(1, NC):
        pl.semaphore_signal(barrier, inc=1, device_id={"col": chip_peer(d)},
                            device_id_type=pl.DeviceIdType.MESH)
    pl.semaphore_signal(barrier, inc=1, device_id={"col": sib},
                        device_id_type=pl.DeviceIdType.MESH)
    pl.semaphore_wait(barrier, R - 1 + NC - 1 + 1)

    sends = []

    def go(copy):
        copy.start()
        sends.append(copy)
        return copy

    feat = {}
    for k in range(K):
        for d in range(R - 1, 0, -1):
            feat[k, d] = go(remote(
                feat_ref.at[:, pl.ds(k * dc, dc)], panel.at[k, r],
                feat_ss.at[k, d], feat_rs.at[k, d], "row", row_peer(d)))
    for k in range(K):
        panel[k, r] = feat_ref[:, k * dc:(k + 1) * dc]

    @pl.loop(0, brows)
    def _(br):
        for p in range(bcols // 2):
            halves = []
            for h in range(2):
                slot = slot_ref[br * bcols + 2 * p + h]
                live = jnp.where(slot >= 0, 1.0, 0.0).astype(F32)
                block = vals_ref[jnp.maximum(slot, 0)]
                halves.append(block.astype(F32) * live)
            pair = jnp.concatenate(halves, axis=1).astype(BF16)
            dense[pl.ds(pl.multiple_of(br * SIDE, SIDE), SIDE), p * 128:(p + 1) * 128] = pair

    @pl.loop(0, brows * SIDE // 128)
    def _(i):
        at = pl.ds(pl.multiple_of(i * 128, 128), 128)
        dense_t[:, at] = dense[at, :].astype(F32).T.astype(BF16)

    ab = {}
    for k in range(K):
        for d in range(1, R):
            feat[k, d].wait_recv()

        def product(piece):
            at = pl.ds(pl.multiple_of(piece * rows, 64), rows)
            return jnp.dot(dense[at, :], panel[k].reshape(R * rows, dc),
                           preferred_element_type=F32)

        @pl.loop(0, NC)
        def _(q):
            a_send[k, q] = product(2 * q + other).astype(BF16)

        a_copy = go(remote(a_send.at[k], a_recv.at[k], a_ss.at[k], a_rs.at[k], "col", sib))

        @pl.loop(0, NC)
        def _(q):
            own[q] = product(2 * q + core)

        a_copy.wait_recv()
        for d in range(NC - 1, -1, -1):
            q = (chip + d) % NC
            total = own[q] + a_recv[k, q].astype(F32)
            if d == 0:
                own[q] = total
                agg_ref[:, k * dc:(k + 1) * dc] = total
            else:
                b_send[k, q] = total.astype(BF16)
                ab[k, d] = go(remote(b_send.at[k, q], b_recv.at[k, d],
                                     b_ss.at[k, d], b_rs.at[k, d], "col", chip_peer(d)))
    for k in range(K):
        total = agg_ref[:, k * dc:(k + 1) * dc]
        for d in range(1, NC):
            ab[k, d].wait_recv()
            total = total + b_recv[k, d].astype(F32)
        agg_ref[:, k * dc:(k + 1) * dc] = total

    agg = agg_ref[...].astype(BF16)
    pre = jnp.dot(agg, w_ref[...], preferred_element_type=F32)
    sig = jax.nn.sigmoid(pre)
    act_ref[...] = (pre * sig).astype(BF16)
    gpre_ref[...] = (og_ref[...].astype(F32) * sig * (1.0 + pre * (1.0 - sig))).astype(BF16)

    hop, direct = {}, {}
    for k in range(K):
        gfull[k, c] = lax.dot_general(
            gpre_ref[...], w_ref[k * dc:(k + 1) * dc, :], (((1,), (1,)), ((), ())),
            preferred_element_type=F32).astype(BF16)
        for d in range(NC - 1, 0, -1):
            direct[k, d] = go(remote(gfull.at[k, c], gfull.at[k, c],
                                     g_ss.at[k, d], g_rs.at[k, d], "col", chip_peer(d)))
        hop[k, 0] = go(remote(gfull.at[k, c], gfull.at[k, c],
                              gs_ss.at[k, 0], gs_rs.at[k, 0], "col", sib))

    part = width // C
    local = jnp.dot(agg_ref[...].T.astype(BF16), gpre_ref[...], preferred_element_type=F32)
    wg[...] = local.reshape(C, part, width)
    for q in range(NC):
        wa_send[q] = wg[2 * q + other].astype(BF16)
    wa = go(remote(wa_send, wa_recv, wa_ss, wa_rs, "col", sib))
    wa.wait_recv()
    wb = {}
    for d in range(1, NC):
        q = (chip + d) % NC
        wb_send[q] = (wg[2 * q + core] + wa_recv[q].astype(F32)).astype(BF16)
        wb[d] = go(remote(wb_send.at[q], wb_recv.at[d], wb_ss.at[d], wb_rs.at[d],
                          "col", chip_peer(d)))

    fr, wzc = {}, {}
    for k in range(K):
        for d in range(1, NC):
            direct[k, d].wait_recv()
            src = 2 * ((chip + NC - d) % NC) + core
            hop[k, d] = go(remote(gfull.at[k, src], gfull.at[k, src],
                                  gs_ss.at[k, d], gs_rs.at[k, d], "col", sib))
        for d in range(NC):
            hop[k, d].wait_recv()

        def back(piece):
            at = pl.ds(pl.multiple_of(piece * rows, 64), rows)
            return jnp.dot(dense_t[at, :], gfull[k].reshape(C * rows, dc),
                           preferred_element_type=F32)

        for d in range(R - 1, -1, -1):
            t = row_peer(d)
            if d:
                f_send[k, d] = back(t).astype(BF16)
                fr[k, d] = go(remote(f_send.at[k, d], f_recv.at[k, d],
                                     f_ss.at[k, d], f_rs.at[k, d], "row", t))
            else:
                own[k] = back(t)

        if k == 0:
            total = wg[c] + wa_recv[chip].astype(F32)
            for d in range(1, NC):
                wb[d].wait_recv()
                total = total + wb_recv[d].astype(F32)
            wz[r] = total.astype(BF16)
            for d in range(R - 1, 0, -1):
                wzc[d] = go(remote(wz.at[r], wz.at[r], wz_ss.at[d], wz_rs.at[d],
                                   "row", row_peer(d)))

    for d in range(1, R):
        wzc[d].wait_recv()
    total = wz[0].astype(F32)
    for i in range(1, R):
        total = total + wz[i].astype(F32)
    wfull[c] = total.astype(BF16)
    wd, wh = {}, {}
    for d in range(NC - 1, 0, -1):
        wd[d] = go(remote(wfull.at[c], wfull.at[c], wh_ss.at[d], wh_rs.at[d],
                          "col", chip_peer(d)))
    wh[0] = go(remote(wfull.at[c], wfull.at[c], ws_ss.at[0], ws_rs.at[0], "col", sib))
    for d in range(1, NC):
        wd[d].wait_recv()
        src = 2 * ((chip + NC - d) % NC) + core
        wh[d] = go(remote(wfull.at[src], wfull.at[src], ws_ss.at[d], ws_rs.at[d], "col", sib))
    for d in range(NC):
        wh[d].wait_recv()
    for i in range(C):
        wgrad_ref[i * part:(i + 1) * part, :] = wfull[i].astype(F32) * scale

    for k in range(K):
        total = own[k]
        for d in range(1, R):
            fr[k, d].wait_recv()
            total = total + f_recv[k, d].astype(F32)
        fgrad_ref[:, k * dc:(k + 1) * dc] = total.astype(BF16)

    for copy in sends:
        copy.wait_send()


def per_device(features, out_grad, weight, block_values, block_coords, block_counts):
    R = lax.axis_size("row")
    C = lax.axis_size("col")
    rows, width = features.shape
    slots = block_values.shape[2]
    brows = rows * C // SIDE
    bcols = rows * R // SIDE
    NC = C // 2
    K = CHUNKS
    dc = width // K
    part = width // C
    ids = jnp.arange(slots, dtype=jnp.int32)
    place = block_coords[0, 0, 0] * bcols + block_coords[0, 0, 1]
    place = jnp.where(ids < block_counts[0, 0], place, -1)
    at = jnp.arange(brows * bcols, dtype=jnp.int32)
    slot_of = jnp.max(jnp.where(place[None, :] == at[:, None], ids[None, :], -1), axis=1)
    vals = block_values.reshape(slots, SIDE, SIDE)
    scale = 1.0 / math.sqrt(rows * R * C)
    vmem = pl.BlockSpec(memory_space=pltpu.VMEM)
    dma = pltpu.SemaphoreType.DMA
    return pl.pallas_call(
        functools.partial(kernel, R, C, scale),
        out_shape=(
            jax.ShapeDtypeStruct((rows, width), BF16),
            jax.ShapeDtypeStruct((width, width), F32),
            jax.ShapeDtypeStruct((rows, width), BF16),
        ),
        in_specs=[pl.BlockSpec(memory_space=pltpu.SMEM), vmem, vmem, vmem, vmem],
        out_specs=(vmem, vmem, vmem),
        scratch_shapes=[
            pltpu.VMEM((brows * SIDE, bcols * SIDE), BF16),
            pltpu.VMEM((bcols * SIDE, brows * SIDE), BF16),
            pltpu.VMEM((K, R, rows, dc), BF16),
            pltpu.VMEM((NC, rows, dc), F32),
            pltpu.VMEM((K, NC, rows, dc), BF16),
            pltpu.VMEM((K, NC, rows, dc), BF16),
            pltpu.VMEM((K, NC, rows, dc), BF16),
            pltpu.VMEM((K, NC, rows, dc), BF16),
            pltpu.VMEM((rows, width), F32),
            pltpu.VMEM((rows, width), BF16),
            pltpu.VMEM((K, C, rows, dc), BF16),
            pltpu.VMEM((K, R, rows, dc), BF16),
            pltpu.VMEM((K, R, rows, dc), BF16),
            pltpu.VMEM((C, part, width), F32),
            pltpu.VMEM((NC, part, width), BF16),
            pltpu.VMEM((NC, part, width), BF16),
            pltpu.VMEM((NC, part, width), BF16),
            pltpu.VMEM((NC, part, width), BF16),
            pltpu.VMEM((R, part, width), BF16),
            pltpu.VMEM((C, part, width), BF16),
            dma((K, R)), dma((K, R)),
            dma((K,)), dma((K,)),
            dma((K, NC)), dma((K, NC)),
            dma((K, NC)), dma((K, NC)),
            dma((K, NC)), dma((K, NC)),
            dma((K, R)), dma((K, R)),
            dma, dma,
            dma((NC,)), dma((NC,)),
            dma((R,)), dma((R,)),
            dma((NC,)), dma((NC,)),
            dma((NC,)), dma((NC,)),
        ],
        compiler_params=pltpu.CompilerParams(
            collective_id=0, has_side_effects=True, vmem_limit_bytes=60 * 1024 * 1024
        ),
    )(slot_of, features, out_grad, weight, vals)


def solution(mesh):
    return jax.shard_map(
        per_device,
        mesh=mesh,
        in_specs=(
            P(("col", "row"), None),
            P(("row", "col"), None),
            P(),
            P("row", "col", None, None),
            P("row", "col", None, None),
            P("row", "col"),
        ),
        out_specs=(P(("row", "col"), None), P(), P(("col", "row"), None)),
        check_vma=False,
    )
```

```python
import functools
import math

import jax
import jax.numpy as jnp
from jax import lax
from jax.experimental import pallas as pl
from jax.experimental.pallas import tpu as pltpu
from jax.sharding import PartitionSpec as P

SIDE = 64
CHUNKS = 4
F32 = jnp.float32
BF16 = jnp.bfloat16


def kernel(
    R, C,
    slot_ref, feat_ref, og_ref, w_ref, vals_ref,
    act_ref, wgrad_ref, fgrad_ref,
    dense, dense_t, panel, own, a_send, a_recv, b_send, b_recv, agg_ref, gpre_ref,
    gfull, f_own, f_total, f_send, f_recv, wg, wa_send, wa_recv, wb_send, wb_recv, wz, wfull,
    feat_ss, feat_rs, a_ss, a_rs, b_ss, b_rs, g_ss, g_rs, gs_ss, gs_rs, f_ss, f_rs,
    wa_ss, wa_rs, wb_ss, wb_rs, wz_ss, wz_rs, wh_ss, wh_rs, ws_ss, ws_rs,
):
    K = CHUNKS
    rows, width = feat_ref.shape
    dc = width // K
    NC = C // 2
    r = lax.axis_index("row")
    c = lax.axis_index("col")
    chip = c // 2
    core = c % 2
    other = 1 - core
    sib = 2 * chip + other
    brows = rows * C // SIDE
    bcols = rows * R // SIDE

    def row_peer(d):
        return (r + d) % R

    def chip_peer(d):
        return 2 * ((chip + d) % NC) + core

    def remote(src, dst, ss, rs, axis, peer):
        return pltpu.make_async_remote_copy(
            src_ref=src, dst_ref=dst, send_sem=ss, recv_sem=rs,
            device_id={axis: peer}, device_id_type=pl.DeviceIdType.MESH,
        )

    barrier = pltpu.get_barrier_semaphore()
    for d in range(1, R):
        pl.semaphore_signal(barrier, inc=1, device_id={"row": row_peer(d)},
                            device_id_type=pl.DeviceIdType.MESH)
    for d in range(1, NC):
        pl.semaphore_signal(barrier, inc=1, device_id={"col": chip_peer(d)},
                            device_id_type=pl.DeviceIdType.MESH)
    pl.semaphore_signal(barrier, inc=1, device_id={"col": sib},
                        device_id_type=pl.DeviceIdType.MESH)
    pl.semaphore_wait(barrier, R - 1 + NC - 1 + 1)

    sends = []

    def go(copy):
        copy.start()
        sends.append((None, copy))
        return copy

    def go_if(cond, copy):
        @pl.when(cond)
        def _():
            copy.start()
        sends.append((cond, copy))
        return copy

    def wait_if(cond, copy):
        @pl.when(cond)
        def _():
            copy.wait_recv()

    right, left = (r + 1) % R, (r + R - 1) % R

    def feature_send(k, s):
        for way in range(2):
            if way == 0:
                cond, origin, peer = (r < R - 1) & (r - s + 1 >= 0), (r + R - s + 1) % R, right
            else:
                cond, origin, peer = (r > 0) & (r + s - 1 <= R - 1), (r + s - 1) % R, left
            src = feat_ref.at[:, pl.ds(k * dc, dc)] if s == 1 else panel.at[k, origin]
            go_if(cond, remote(src, panel.at[k, origin], feat_ss.at[way, k, s],
                               feat_rs.at[way, k, s], "row", peer))

    def feature_wait(k, s):
        for way in range(2):
            if way == 0:
                cond, origin, peer = r - s >= 0, (r + R - s) % R, left
            else:
                cond, origin, peer = r + s <= R - 1, (r + s) % R, right
            wait_if(cond, remote(panel.at[k, origin], panel.at[k, origin],
                                 feat_ss.at[way, k, s], feat_rs.at[way, k, s], "row", peer))

    def feature_diagonal(t):
        for k in range(K):
            s = t - k
            if 2 <= s <= R:
                feature_wait(k, s - 1)
            if 1 <= s <= R - 1:
                feature_send(k, s)

    feature_diagonal(1)
    for k in range(K):
        panel[k, r] = feat_ref[:, k * dc:(k + 1) * dc]

    @pl.loop(0, brows)
    def _(br):
        for p in range(bcols // 2):
            halves = []
            for h in range(2):
                slot = slot_ref[br * bcols + 2 * p + h]
                live = jnp.where(slot >= 0, 1.0, 0.0).astype(F32)
                block = vals_ref[jnp.maximum(slot, 0)]
                halves.append(block.astype(F32) * live)
            pair = jnp.concatenate(halves, axis=1).astype(BF16)
            dense[pl.ds(pl.multiple_of(br * SIDE, SIDE), SIDE), p * 128:(p + 1) * 128] = pair

    @pl.loop(0, brows * SIDE // 128)
    def _(i):
        at = pl.ds(pl.multiple_of(i * 128, 128), 128)
        dense_t[:, at] = dense[at, :].astype(F32).T.astype(BF16)

    ab, pair_copy = {}, {}

    def product(k, piece):
        at = pl.ds(pl.multiple_of(piece * rows, 64), rows)
        return jnp.dot(dense[at, :], panel[k].reshape(R * rows, dc),
                       preferred_element_type=F32)

    def pair_sum(k):
        pair_copy[k].wait_recv()
        for d in range(NC - 1, -1, -1):
            q = (chip + d) % NC
            total = own[q] + a_recv[k, q].astype(F32)
            if d == 0:
                agg_ref[:, k * dc:(k + 1) * dc] = total
            else:
                b_send[k, q] = total.astype(BF16)
                ab[k, d] = go(remote(b_send.at[k, q], b_recv.at[k, d],
                                     b_ss.at[k, d], b_rs.at[k, d], "col", chip_peer(d)))

    for t in range(2, R + K):
        feature_diagonal(t)
        k = t - R
        if k >= 0:
            @pl.loop(0, NC)
            def _(q):
                a_send[k, q] = product(k, 2 * q + other).astype(BF16)

            pair_copy[k] = go(remote(a_send.at[k], a_recv.at[k], a_ss.at[k], a_rs.at[k],
                                     "col", sib))
            if k > 0:
                pair_sum(k - 1)

            @pl.loop(0, NC)
            def _(q):
                own[q] = product(k, 2 * q + core)
    pair_sum(K - 1)
    for k in range(K):
        total = agg_ref[:, k * dc:(k + 1) * dc]
        for d in range(1, NC):
            ab[k, d].wait_recv()
            total = total + b_recv[k, d].astype(F32)
        agg_ref[:, k * dc:(k + 1) * dc] = total

    agg = agg_ref[...].astype(BF16)
    pre = jnp.dot(agg, w_ref[...], preferred_element_type=F32)
    sig = jax.nn.sigmoid(pre)
    act_ref[...] = (pre * sig).astype(BF16)
    gpre_ref[...] = (og_ref[...].astype(F32) * sig * (1.0 + pre * (1.0 - sig))).astype(BF16)

    hop, direct, wb = {}, {}, {}
    part = width // C
    for k in range(K):
        gfull[k, c] = lax.dot_general(
            gpre_ref[...], w_ref[k * dc:(k + 1) * dc, :], (((1,), (1,)), ((), ())),
            preferred_element_type=F32).astype(BF16)
        for d in range(NC - 1, 0, -1):
            direct[k, d] = go(remote(gfull.at[k, c], gfull.at[k, c],
                                     g_ss.at[k, d], g_rs.at[k, d], "col", chip_peer(d)))
        hop[k, 0] = go(remote(gfull.at[k, c], gfull.at[k, c],
                              gs_ss.at[k, 0], gs_rs.at[k, 0], "col", sib))
        if k == 1:
            local = jnp.dot(agg_ref[...].T.astype(BF16), gpre_ref[...],
                            preferred_element_type=F32)
            wg[...] = local.reshape(C, part, width)
            for q in range(NC):
                wa_send[q] = wg[2 * q + other].astype(BF16)
            wa = go(remote(wa_send, wa_recv, wa_ss, wa_rs, "col", sib))
        if k == 2:
            wa.wait_recv()
            for d in range(1, NC):
                q = (chip + d) % NC
                wb_send[q] = (wg[2 * q + core] + wa_recv[q].astype(F32)).astype(BF16)
                wb[d] = go(remote(wb_send.at[q], wb_recv.at[d], wb_ss.at[d], wb_rs.at[d],
                                  "col", chip_peer(d)))

    wzc = {}

    def tail_copy(way, k, t, peer):
        return remote(f_send.at[way, k, t], f_recv.at[way, k, t],
                      f_ss.at[way, k, t], f_rs.at[way, k, t], "row", peer)

    def tail_send(k, s, way):
        at_r = s if way == 0 else R - 1 - s
        targets = range(R - 1, at_r, -1) if way == 0 else range(0, at_r)

        @pl.when(r == at_r)
        def _():
            for t in targets:
                total = f_own[k, t]
                if s:
                    tail_copy(way, k, t, left if way == 0 else right).wait_recv()
                    total = total + f_recv[way, k, t].astype(F32)
                f_send[way, k, t] = total.astype(BF16)
                tail_copy(way, k, t, right if way == 0 else left).start()

    for tau in range(K + R - 2):
        if tau < K:
            k = tau
            for d in range(1, NC):
                direct[k, d].wait_recv()
                src = 2 * ((chip + NC - d) % NC) + core
                hop[k, d] = go(remote(gfull.at[k, src], gfull.at[k, src],
                                      gs_ss.at[k, d], gs_rs.at[k, d], "col", sib))
            for d in range(NC):
                hop[k, d].wait_recv()

            @pl.loop(0, R)
            def _(t):
                at = pl.ds(pl.multiple_of(t * rows, 64), rows)
                f_own[k, t] = jnp.dot(dense_t[at, :], gfull[k].reshape(C * rows, dc),
                                      preferred_element_type=F32)

        for s in range(R - 1):
            if 0 <= tau - s < K:
                tail_send(tau - s, s, 0)
                tail_send(tau - s, s, 1)

        if tau == 2:
            total = wg[c] + wa_recv[chip].astype(F32)
            for d in range(1, NC):
                wb[d].wait_recv()
                total = total + wb_recv[d].astype(F32)
            wz[r] = total.astype(BF16)
            for d in range(R - 1, 0, -1):
                wzc[d] = go(remote(wz.at[r], wz.at[r], wz_ss.at[d], wz_rs.at[d],
                                   "row", row_peer(d)))

    for d in range(1, R):
        wzc[d].wait_recv()
    total = wz[0].astype(F32)
    for i in range(1, R):
        total = total + wz[i].astype(F32)
    wfull[c] = total.astype(BF16)
    wd, wh = {}, {}
    for d in range(NC - 1, 0, -1):
        wd[d] = go(remote(wfull.at[c], wfull.at[c], wh_ss.at[d], wh_rs.at[d],
                          "col", chip_peer(d)))
    wh[0] = go(remote(wfull.at[c], wfull.at[c], ws_ss.at[0], ws_rs.at[0], "col", sib))
    for d in range(1, NC):
        wd[d].wait_recv()
        src = 2 * ((chip + NC - d) % NC) + core
        wh[d] = go(remote(wfull.at[src], wfull.at[src], ws_ss.at[d], ws_rs.at[d], "col", sib))
    for d in range(NC):
        wh[d].wait_recv()
    for i in range(C):
        wgrad_ref[i * part:(i + 1) * part, :] = wfull[i]

    for k in range(K):
        f_total[...] = f_own[k, r]
        for way in range(2):
            @pl.when(r > 0 if way == 0 else r < R - 1)
            def _():
                tail_copy(way, k, r, left if way == 0 else right).wait_recv()
                f_total[...] += f_recv[way, k, r].astype(F32)
        fgrad_ref[:, k * dc:(k + 1) * dc] = f_total[...].astype(BF16)

    for k in range(K):
        for t in range(R):
            @pl.when(r < t)
            def _():
                tail_copy(0, k, t, right).wait_send()

            @pl.when(r > t)
            def _():
                tail_copy(1, k, t, left).wait_send()
    for cond, copy in sends:
        if cond is None:
            copy.wait_send()
        else:
            @pl.when(cond)
            def _():
                copy.wait_send()


def per_device(features, out_grad, weight, block_values, block_coords, block_counts):
    R = lax.axis_size("row")
    C = lax.axis_size("col")
    rows, width = features.shape
    slots = block_values.shape[2]
    brows = rows * C // SIDE
    bcols = rows * R // SIDE
    NC = C // 2
    K = CHUNKS
    dc = width // K
    part = width // C
    ids = jnp.arange(slots, dtype=jnp.int32)
    place = block_coords[0, 0, 0] * bcols + block_coords[0, 0, 1]
    place = jnp.where(ids < block_counts[0, 0], place, -1)
    at = jnp.arange(brows * bcols, dtype=jnp.int32)
    slot_of = jnp.max(jnp.where(place[None, :] == at[:, None], ids[None, :], -1), axis=1)
    vals = block_values.reshape(slots, SIDE, SIDE)
    scale = 1.0 / math.sqrt(rows * R * C)
    vmem = pl.BlockSpec(memory_space=pltpu.VMEM)
    dma = pltpu.SemaphoreType.DMA
    activations, wsum, feature_grad = pl.pallas_call(
        functools.partial(kernel, R, C),
        out_shape=(
            jax.ShapeDtypeStruct((rows, width), BF16),
            jax.ShapeDtypeStruct((width, width), BF16),
            jax.ShapeDtypeStruct((rows, width), BF16),
        ),
        in_specs=[pl.BlockSpec(memory_space=pltpu.SMEM), vmem, vmem, vmem, vmem],
        out_specs=(vmem, vmem, vmem),
        scratch_shapes=[
            pltpu.VMEM((brows * SIDE, bcols * SIDE), BF16),
            pltpu.VMEM((bcols * SIDE, brows * SIDE), BF16),
            pltpu.VMEM((K, R, rows, dc), BF16),
            pltpu.VMEM((NC, rows, dc), F32),
            pltpu.VMEM((K, NC, rows, dc), BF16),
            pltpu.VMEM((K, NC, rows, dc), BF16),
            pltpu.VMEM((K, NC, rows, dc), BF16),
            pltpu.VMEM((K, NC, rows, dc), BF16),
            pltpu.VMEM((rows, width), F32),
            pltpu.VMEM((rows, width), BF16),
            pltpu.VMEM((K, C, rows, dc), BF16),
            pltpu.VMEM((K, R, rows, dc), F32),
            pltpu.VMEM((rows, dc), F32),
            pltpu.VMEM((2, K, R, rows, dc), BF16),
            pltpu.VMEM((2, K, R, rows, dc), BF16),
            pltpu.VMEM((C, part, width), F32),
            pltpu.VMEM((NC, part, width), BF16),
            pltpu.VMEM((NC, part, width), BF16),
            pltpu.VMEM((NC, part, width), BF16),
            pltpu.VMEM((NC, part, width), BF16),
            pltpu.VMEM((R, part, width), BF16),
            pltpu.VMEM((C, part, width), BF16),
            dma((2, K, R)), dma((2, K, R)),
            dma((K,)), dma((K,)),
            dma((K, NC)), dma((K, NC)),
            dma((K, NC)), dma((K, NC)),
            dma((K, NC)), dma((K, NC)),
            dma((2, K, R)), dma((2, K, R)),
            dma, dma,
            dma((NC,)), dma((NC,)),
            dma((R,)), dma((R,)),
            dma((NC,)), dma((NC,)),
            dma((NC,)), dma((NC,)),
        ],
        compiler_params=pltpu.CompilerParams(
            collective_id=0, has_side_effects=True, vmem_limit_bytes=60 * 1024 * 1024
        ),
    )(slot_of, features, out_grad, weight, vals)
    return activations, wsum.astype(F32) * F32(scale), feature_grad


def solution(mesh):
    return jax.shard_map(
        per_device,
        mesh=mesh,
        in_specs=(
            P(("col", "row"), None),
            P(("row", "col"), None),
            P(),
            P("row", "col", None, None),
            P("row", "col", None, None),
            P("row", "col"),
        ),
        out_specs=(P(("row", "col"), None), P(), P(("col", "row"), None)),
        check_vma=False,
    )
```
